512 devices in a mesh: row: 32 (over x_lo, z, core), col: 16 (over y, x_hi).
Axes of the slice: x: 4 (x_hi: 2, x_lo: 2; x = x_hi * 2 + x_lo), y: 8, z: 8, core: 2. Of those that a mesh axis runs over, the one named last changes fastest.
Arguments:
- patches: bfloat16 [512, 256, 512], P('row', 'col'), may hold values from -6 to 6
- cotangent: bfloat16 [512, 256, 512], P('row', 'col'), may hold values from -6 to 6
- mask_map: int32 [512, 256], P('row', 'col'), may hold values from 0 to 1, as said below
- mask_token: bfloat16 [512], replicated, may hold values from -5 to 5
- w_qkv: bfloat16 [512, 1536], replicated, may hold values from -0.25 to 0.25
- w_proj: bfloat16 [512, 512], replicated, may hold values from -0.25 to 0.25
- proj_bias: float32 [512], replicated, may hold values from -3 to 3
- norm_gain: float32 [512], replicated, may hold values from 0.1 to 1.9
- scales: float32 [16], replicated, may hold values from 2 to 24
- bias_table: float32 [961, 16], replicated, may hold values from 0 to 6
- rel_index: int32 [256, 256], replicated, may hold values from 0 to 960, as said below
Outputs:
- grad_input: bfloat16 [512, 256, 512], P('row', 'col')
The draws below stay inside these ranges and needn't reach their ends.
Inputs may be any that keep to these rules, and one draw needn't show every extreme that they name: mask_map is constant on aligned 8 x 8 blocks of patches. rel_index[t, s] = sigma((row_t - row_s + 15) * 31 + col_t - col_s + 15) for a bijection sigma of 0 to 960, where row and col are a token's position inside its window.
All inputs are finite; a program needn't handle non-finite values.
Results may differ from the reference program's by a relative error of at most 0.022.
Values may be sent and summed in bfloat16 or wider, within the bound.
No kernel may reach another device: no remote copies, remote signals or barrier semaphores. Data moves between devices by JAX's collectives and lax.ppermute only.
A program may use at most 128 MiB of HBM per device.

```python
import math
import jax
import jax.numpy as jnp
from jax import lax

D = 512
HEADS = 16
WIN = 16
SHIFT = 8
BIAS_ROWS = 961
MASK_BLOCK = 8
NH = 512
NW = 256


def draw_mask_map(key, part):
    key = jax.random.fold_in(key, 11)
    blocks = jax.random.randint(key, (NH // MASK_BLOCK, NW // MASK_BLOCK), 0, 5)
    chosen = (blocks < 3).astype(jnp.int32)
    return jnp.repeat(jnp.repeat(chosen, MASK_BLOCK, axis=0), MASK_BLOCK, axis=1)


def draw_rel_index(key, part):
    key = jax.random.fold_in(key, 23)
    places = jnp.arange(WIN * WIN, dtype=jnp.int32)
    place_rows = places // WIN
    place_cols = places % WIN
    offset = (place_rows[:, None] - place_rows[None, :] + WIN - 1) * (2 * WIN - 1) + (place_cols[:, None] - place_cols[None, :] + WIN - 1)
    relabel = jax.random.permutation(key, BIAS_ROWS).astype(jnp.int32)
    return relabel[offset].astype(jnp.int32)


def block_scale(rng, shape, pieces, least, top_value):
    def one(axis_at, shards_of):
        heights = jax.random.uniform(jax.random.fold_in(jax.random.fold_in(rng, 6), axis_at), (shards_of,), jnp.float32, least / len(pieces), top_value / len(pieces))
        return jnp.repeat(jnp.exp(heights), shape[axis_at] // shards_of).reshape((-1,) + (1,) * (len(shape) - axis_at - 1))

    loudness = one(*pieces[0])
    for cut in pieces[1:]:
        loudness = loudness * one(*cut)
    return loudness


def normal_values(stream_key, shape, scale, limit, split=(), held_as=jnp.bfloat16):
    values = scale * jax.random.normal(stream_key, shape, jnp.float32)
    if split:
        values = values * block_scale(stream_key, shape, split, -0.22, 0.18)
    return jnp.clip(values, -limit, limit).astype(held_as)


def setup_inputs(seed: int = 0) -> dict:
    splits = jax.random.split(jax.random.key(seed), 12)
    patches = normal_values(splits[0], (NH, NW, D), 1.0, 6.0, ((0, 32), (1, 16)))
    cotangent = normal_values(splits[1], (NH, NW, D), 1.0, 6.0, ((0, 32), (1, 16)))
    mask_map = draw_mask_map(jax.random.fold_in(splits[11], 71), 0)
    mask_token = normal_values(splits[3], (D,), 1.0, 5.0)
    w_qkv = normal_values(splits[4], (D, 3 * D), D ** -0.5, 0.25)
    w_proj = normal_values(splits[5], (D, D), D ** -0.5, 0.25)
    proj_bias = normal_values(splits[6], (D,), 0.5, 3.0, (), jnp.float32)
    norm_gain = jnp.clip(1.0 + 0.18 * jax.random.normal(splits[7], (D,), jnp.float32), 0.1, 1.9)
    scales = jnp.clip(jnp.exp(jax.random.uniform(splits[8], (HEADS,), jnp.float32, math.log(2.0), math.log(24.0))), 2.0, 24.0)
    bias_table = jnp.clip(jax.random.uniform(splits[9], (BIAS_ROWS, HEADS), jnp.float32, 0.0, 6.0), 0.0, 6.0)
    rel_index = draw_rel_index(jax.random.fold_in(splits[11], 71), 0)
    return {"patches": patches, "cotangent": cotangent, "mask_map": mask_map, "mask_token": mask_token, "w_qkv": w_qkv, "w_proj": w_proj, "proj_bias": proj_bias, "norm_gain": norm_gain, "scales": scales, "bias_table": bias_table, "rel_index": rel_index}


def to_windows(tile):
    height, breadth, depth = tile.shape
    return tile.reshape(height // WIN, WIN, breadth // WIN, WIN, depth).transpose(0, 2, 1, 3, 4).reshape(-1, WIN * WIN, depth)

def from_windows(windows, height, breadth):
    depth = windows.shape[-1]
    return windows.reshape(height // WIN, breadth // WIN, WIN, WIN, depth).transpose(0, 2, 1, 3, 4).reshape(height, breadth, depth)

def attend(tokens, mask_add, w_qkv, w_proj, proj_bias, norm_gain, scales, bias_heads):
    count, width = tokens.shape
    heads = scales.shape[0]
    packed = jnp.dot(tokens, w_qkv, preferred_element_type=jnp.float32).astype(jnp.bfloat16)
    packed = packed.reshape(count, 3, heads, width // heads)
    query_rows = packed[:, 0].astype(jnp.float32)
    key_rows = packed[:, 1].astype(jnp.float32)
    value_rows = packed[:, 2]
    query_rows = query_rows * lax.rsqrt(lax.optimization_barrier(jnp.sum(query_rows * query_rows, axis=-1, keepdims=True)) + 1e-06)
    key_rows = key_rows * lax.rsqrt(lax.optimization_barrier(jnp.sum(key_rows * key_rows, axis=-1, keepdims=True)) + 1e-06)
    scores = jnp.einsum('qhd,khd->hqk', query_rows, key_rows, precision=lax.Precision.HIGHEST)
    scores = scores * scales[:, None, None] + bias_heads + mask_add[None]
    raised = jnp.exp(scores)
    weights = (raised / lax.optimization_barrier(jnp.sum(raised, axis=-1, keepdims=True))).astype(jnp.bfloat16)
    attended = jnp.einsum('hqk,khd->qhd', weights.astype(jnp.float32), value_rows.astype(jnp.float32))
    attended = attended.astype(jnp.bfloat16).reshape(count, width)
    projected = jnp.dot(attended, w_proj, preferred_element_type=jnp.float32) + proj_bias
    centre = lax.optimization_barrier(jnp.mean(projected, axis=-1, keepdims=True))
    centered = projected - centre
    spread = lax.optimization_barrier(jnp.mean(centered * centered, axis=-1, keepdims=True))
    return centered * lax.rsqrt(spread + 1e-05) * norm_gain

def reference(patches, cotangent, mask_map, mask_token, w_qkv, w_proj, proj_bias, norm_gain, scales, bias_table, rel_index):
    masked = (mask_map == 1)[:, :, None]
    mixed = jnp.where(masked, mask_token[None, None, :], patches)
    shifted = jnp.roll(mixed, (-SHIFT, -SHIFT), axis=(0, 1))
    ahead = jnp.roll(cotangent, (-SHIFT, -SHIFT), axis=(0, 1))
    grid_rows = jnp.arange(NH, dtype=jnp.int32)
    grid_cols = jnp.arange(NW, dtype=jnp.int32)
    band_rows = (grid_rows >= NH - WIN).astype(jnp.int32) + (grid_rows >= NH - SHIFT).astype(jnp.int32)
    band_cols = (grid_cols >= NW - WIN).astype(jnp.int32) + (grid_cols >= NW - SHIFT).astype(jnp.int32)
    region = 3 * band_rows[:, None] + band_cols[None, :]
    window_rows = NH // WIN
    window_cols = NW // WIN
    region_windows = to_windows(region[:, :, None])[:, :, 0].reshape(window_rows, window_cols, WIN * WIN)
    token_windows = to_windows(shifted).reshape(window_rows, window_cols, WIN * WIN, D)
    grad_windows = to_windows(ahead).reshape(window_rows, window_cols, WIN * WIN, D)
    bias_heads = jnp.transpose(bias_table[rel_index], (2, 0, 1))

    def one_window(tokens, incoming, region_row):
        mask_add = jnp.where(region_row[:, None] == region_row[None, :], jnp.float32(0.0), jnp.float32(-100.0))
        result, pullback = jax.vjp(lambda inputs: attend(inputs, mask_add, w_qkv, w_proj, proj_bias, norm_gain, scales, bias_heads), tokens)
        return pullback(incoming.astype(jnp.float32))[0]

    def one_band(packed_in):
        return jax.vmap(one_window)(packed_in[0], packed_in[1], packed_in[2])
    returned = lax.map(one_band, (token_windows, grad_windows, region_windows))
    grad_shifted = from_windows(returned.reshape(window_rows * window_cols, WIN * WIN, D), NH, NW)
    behind = jnp.roll(grad_shifted, (SHIFT, SHIFT), axis=(0, 1))
    total = cotangent.astype(jnp.float32) + behind.astype(jnp.float32)
    return jnp.where(masked, jnp.float32(0.0), total).astype(jnp.bfloat16)
```

```python
import math

import jax
import jax.numpy as jnp
from jax import lax
from jax.experimental import pallas as pl
from jax.experimental.pallas import tpu as pltpu
from jax.sharding import PartitionSpec as P

WIN = 16
HALF = 8
QUART = HALF * HALF
TOK = WIN * WIN
D = 512
HEADS = 16
HD = D // HEADS
BIAS_ROWS = 961
LOG2E = math.log2(math.e)
F32 = jnp.float32
BF16 = jnp.bfloat16


def dot(a, b, ca, cb):
    return lax.dot_general(a, b, (((ca,), (cb,)), ((), ())), preferred_element_type=F32)


def hidden_at(mask_ref, r, c):
    return jnp.broadcast_to(mask_ref[r * HALF : r * HALF + 1, c * HALF : c * HALF + 1], (QUART, D)) == 1


def mixed_piece(mask_ref, patches_ref, token_ref, r, c):
    piece = patches_ref[r * HALF : (r + 1) * HALF, c * HALF : (c + 1) * HALF, :].reshape(QUART, D)
    token = jnp.broadcast_to(token_ref[...].reshape(1, D), (QUART, D))
    return jnp.where(hidden_at(mask_ref, r, c), token, piece)


def raw_piece(ref, r, c):
    return ref[r * HALF : (r + 1) * HALF, c * HALF : (c + 1) * HALF, :].reshape(QUART, D)


def prep_kernel(mask_ref, patches_ref, cot_ref, token_ref, diag_ref, right_ref, below_ref):
    for (r, c, out_ref) in ((1, 0, right_ref), (0, 0, diag_ref), (0, 1, below_ref)):
        out_ref[:QUART, :] = mixed_piece(mask_ref, patches_ref, token_ref, r, c)
        out_ref[QUART:, :] = raw_piece(cot_ref, r, c)


def prep(mask_map, patches, cotangent, token):
    vmem = pl.BlockSpec(memory_space=pltpu.VMEM)
    return pl.pallas_call(
        prep_kernel,
        out_shape=[jax.ShapeDtypeStruct((2 * QUART, D), BF16)] * 3,
        in_specs=[vmem] * 4,
        out_specs=[vmem] * 3,
        name="prep",
    )(mask_map, patches, cotangent, token)


def bias_kernel(edge_ref, rel_ref, table_ref, out_ref, table_pad, base):
    ends = jnp.concatenate([rel_ref[:, 0:128].T, rel_ref[:, 128:256].T], axis=0)
    fixed = jnp.concatenate([ends[255:256], ends[15:16], ends[240:241], ends[0:1]] * 2, axis=0)
    high_part = fixed // 8
    row8 = lax.broadcasted_iota(jnp.int32, (8, TOK), 0)
    digits = jnp.where(row8 < 4, high_part, fixed - high_part * 8).astype(F32).astype(BF16)

    table_pad[...] = jnp.zeros_like(table_pad)
    scaled = table_ref[...] * LOG2E
    high = scaled.astype(BF16)
    table_pad[:HEADS, :BIAS_ROWS] = high.astype(F32)
    table_pad[HEADS:, :BIAS_ROWS] = scaled - high.astype(F32)
    entries = table_pad.shape[1]
    lane1 = lax.broadcasted_iota(jnp.int32, (1, TOK), 1)
    dr, c = lane1 // 8, lane1 % 8
    for part in range(4):
        col = c + (-1, 7, 0, 8)[part]
        late = dr >= 15
        row = jnp.where(late, dr - 15, dr)
        token = jnp.clip(row * WIN + col, 0, TOK - 1)
        take = lax.broadcasted_iota(jnp.int32, (TOK, TOK), 0) == token
        found = dot(digits, jnp.where(take, 1.0, 0.0).astype(BF16), 1, 0)
        pair = 0 if part < 2 else 2
        order = found[0:4] * 8.0 + found[4:8]
        order = jnp.where(late, order[pair + 1 : pair + 2], order[pair : pair + 1]).astype(jnp.int32)
        chosen = lax.broadcasted_iota(jnp.int32, (entries, TOK), 0) == order
        both = dot(table_pad[...].astype(BF16), jnp.where(chosen, 1.0, 0.0).astype(BF16), 1, 0)
        base[:, part * TOK : (part + 1) * TOK] = both[:HEADS] + both[HEADS:]

    lane = lax.broadcasted_iota(jnp.int32, (8, 256), 1)
    sub = lax.broadcasted_iota(jnp.int32, (8, 256), 0)
    straight = (lane % 8) >= sub
    lane = lax.broadcasted_iota(jnp.int32, (8, 128), 1)
    left = lane < 64
    cut = -100.0 * LOG2E
    row_cut = jnp.where(edge_ref[0] == 1, cut, 0.0)
    col_cut = jnp.where(edge_ref[1] == 1, cut, 0.0)
    masks = {}
    for ch in range(2):
        across = jnp.where(left == (ch == 0), 0.0, col_cut)
        masks[ch, 0] = across
        masks[ch, 1] = jnp.minimum(across, row_cut)

    def swap(v):
        return pltpu.roll(v, 64, 1)

    def head(h, carry):
        strips = [
            jnp.broadcast_to(base[pl.ds(h, 1), pl.ds(d * 256, 256)], (8, 256)) for d in range(4)
        ]
        here = [pltpu.roll(s, 0, 1, stride=1, stride_axis=0) for s in strips[1:]]
        wrapped = [pltpu.roll(s, 248, 1, stride=1, stride_axis=0) for s in strips[:3]]
        fields = [jnp.where(straight, a, b) for a, b in zip(here, wrapped)]
        low = [f[:, :128] for f in fields]
        top = [f[:, 128:] for f in fields]
        low_s = [swap(v) for v in low]
        top_s = [swap(v) for v in top]
        for ch in range(2):
            a, b = 1 - ch, 2 - ch
            first = [
                jnp.where(left, low[a], low_s[b]),
                jnp.where(left, low_s[a], low[b]),
                jnp.where(left, top[a], top_s[b]),
            ]
            second = [
                None,
                jnp.where(left, low_s[b], low[a]),
                jnp.where(left, top[b], top_s[a]),
                jnp.where(left, top_s[b], top[a]),
            ]
            for p in range(24):
                k, r = divmod(p, 8)
                vreg = first[k]
                if r:
                    vreg = jnp.where(lane % 64 >= 8 * r, first[k], second[k + 1])
                    vreg = pltpu.roll(vreg, 128 - 8 * r, 1)
                for rh_t in range(2):
                    for rh_s in range(2):
                        rl_s = 8 * (rh_t - rh_s) + 15 - p
                        if 0 <= rl_s < 8:
                            at = ((rh_s * 2 + ch) * 8 + rl_s) * 8
                            out_ref[h, at : at + 8, rh_t * 128 : (rh_t + 1) * 128] = (
                                vreg + masks[ch, int(rh_t != rh_s)]
                            )
        return carry

    lax.fori_loop(0, HEADS, head, 0, unroll=4)


def build_bias(edge, rel_index, table_t):
    vmem = pl.BlockSpec(memory_space=pltpu.VMEM)
    return pl.pallas_call(
        bias_kernel,
        out_shape=jax.ShapeDtypeStruct((HEADS, TOK, TOK), F32),
        in_specs=[pl.BlockSpec(memory_space=pltpu.SMEM), vmem, vmem],
        out_specs=vmem,
        scratch_shapes=[pltpu.VMEM((2 * HEADS, 1024), F32), pltpu.VMEM((HEADS, 1024), F32)],
        compiler_params=pltpu.CompilerParams(vmem_limit_bytes=24 * 2**20),
        cost_estimate=pl.CostEstimate(flops=2**26, bytes_accessed=2**22, transcendentals=0),
        name="bias",
    )(edge, rel_index, table_t)


def attend_kernel(
    scales_ref, mask_ref, patches_ref, cot_ref, token_ref, diag_ref, right_ref, below_ref,
    wqkv_ref, wproj_ref, pbias_ref, gain_ref,
    bias_ref, own_out, below_out, right_out, diag_out,
    packed, qhat, khat, rnorm, weights, attended, inverse, vaug, dpacked, dattended,
):
    pieces = (right_ref, below_ref, diag_ref)
    own = mixed_piece(mask_ref, patches_ref, token_ref, 1, 1)
    tokens = jnp.concatenate([own] + [ref[:QUART, :] for ref in pieces], axis=0)
    packed[...] = dot(tokens, wqkv_ref[...], 1, 0).astype(BF16).T
    ones = jnp.where(lax.broadcasted_iota(jnp.int32, (16, TOK), 0) < 2, 1.0, 0.0).astype(BF16)

    def score(h):
        rows = slice(h * HD, (h + 1) * HD)
        query = packed[h * HD : (h + 1) * HD, :].astype(F32)
        key = packed[D + h * HD : D + (h + 1) * HD, :].astype(F32)
        rq = lax.rsqrt(jnp.sum(query * query, axis=0, keepdims=True) + 1e-6)
        rk = lax.rsqrt(jnp.sum(key * key, axis=0, keepdims=True) + 1e-6)
        rnorm[h : h + 1, :] = rq
        rnorm[HEADS + h : HEADS + h + 1, :] = rk
        qn = query * rq
        kn = key * rk
        qhat[rows, :] = qn
        khat[rows, :] = kn
        return dot(kn.astype(BF16), (qn * (scales_ref[h] * LOG2E)).astype(BF16), 0, 0)

    def gather(h, raised):
        rows = slice(h * HD, (h + 1) * HD)
        vrows = jnp.concatenate([packed[2 * D + h * HD : 2 * D + (h + 1) * HD, :], ones], axis=0)
        vaug[h] = vrows
        gathered = dot(vrows, raised, 1, 0)
        inv = 1.0 / gathered[HD : HD + 1, :]
        inverse[h : h + 1, :] = inv
        attended[rows, :] = gathered[:HD] * inv

    scores, raised = {}, {}
    for step in range(HEADS + 3):
        if step < HEADS:
            scores[step] = score(step)
        h = step - 1
        if 0 <= h < HEADS:
            raised[h] = jnp.exp2(scores.pop(h) + bias_ref[h]).astype(BF16)
            weights[h] = raised[h]
        h = step - 3
        if 0 <= h < HEADS:
            gather(h, raised.pop(h))

    projected = dot(attended[...].astype(BF16), wproj_ref[...], 0, 0) + pbias_ref[...].reshape(1, D)
    centred = projected - jnp.mean(projected, axis=1, keepdims=True)
    rstd = lax.rsqrt(jnp.mean(centred * centred, axis=1, keepdims=True) + 1e-5)
    xhat = centred * rstd
    ahead = jnp.concatenate([raw_piece(cot_ref, 1, 1)] + [ref[QUART:, :] for ref in pieces], axis=0).astype(F32)
    grad = ahead * gain_ref[...].reshape(1, D)
    grad = rstd * (
        grad
        - jnp.mean(grad, axis=1, keepdims=True)
        - xhat * jnp.mean(grad * xhat, axis=1, keepdims=True)
    )
    dattended[...] = dot(wproj_ref[...], grad.astype(BF16), 1, 1).astype(BF16)

    def spread(h):
        rows = slice(h * HD, (h + 1) * HD)
        da = dattended[rows, :]
        delta = -jnp.sum(da.astype(F32) * attended[rows, :], axis=0, keepdims=True)
        dhigh = delta.astype(BF16).astype(F32)
        tail = jnp.concatenate([dhigh, delta - dhigh, jnp.zeros((14, TOK), F32)], axis=0).astype(BF16)
        return dot(vaug[h], jnp.concatenate([da, tail], axis=0), 0, 0)

    def collect(h, dscores):
        rows = slice(h * HD, (h + 1) * HD)
        inv = inverse[h : h + 1, :]
        qn = qhat[rows, :]
        kn = khat[rows, :]
        scaled = inv * scales_ref[h]
        dv = dot((dattended[rows, :].astype(F32) * inv).astype(BF16), weights[h], 1, 1)
        dq = dot(kn.astype(BF16), dscores, 1, 0) * scaled
        dk = dot((qn * scaled).astype(BF16), dscores, 1, 1)
        return dq, dk, dv

    def finish(h, dq, dk, dv):
        rows = slice(h * HD, (h + 1) * HD)
        qn = qhat[rows, :]
        kn = khat[rows, :]
        dq = rnorm[h : h + 1, :] * (dq - qn * jnp.sum(qn * dq, axis=0, keepdims=True))
        dk = rnorm[HEADS + h : HEADS + h + 1, :] * (dk - kn * jnp.sum(kn * dk, axis=0, keepdims=True))
        dpacked[h * HD : (h + 1) * HD, :] = dq.astype(BF16)
        dpacked[D + h * HD : D + (h + 1) * HD, :] = dk.astype(BF16)
        dpacked[2 * D + h * HD : 2 * D + (h + 1) * HD, :] = dv.astype(BF16)

    dweights, dscores, grads = {}, {}, {}
    for step in range(HEADS + 3 + 1):
        if step < HEADS:
            dweights[step] = spread(step)
        h = step - 1
        if 0 <= h < HEADS:
            dscores[h] = weights[h] * dweights.pop(h).astype(BF16)
        h = step - 3
        if 0 <= h < HEADS:
            grads[h] = collect(h, dscores.pop(h))
        h = step - 3 - 1
        if 0 <= h < HEADS:
            finish(h, *grads.pop(h))

    result = dot(wqkv_ref[...], dpacked[...], 1, 0).astype(BF16).T
    for i, ref in enumerate((own_out, right_out, below_out, diag_out)):
        ref[...] = result[i * QUART : (i + 1) * QUART, :]


def attend(scales, mask_map, patches, cotangent, token, diag, right, below, wqkv, wproj, pbias, gain, bias):
    vmem = pl.BlockSpec(memory_space=pltpu.VMEM)
    return pl.pallas_call(
        attend_kernel,
        out_shape=[jax.ShapeDtypeStruct((QUART, D), BF16)] * 4,
        in_specs=[pl.BlockSpec(memory_space=pltpu.SMEM)] + [vmem] * 12,
        out_specs=[vmem] * 4,
        scratch_shapes=[
            pltpu.VMEM((3 * D, TOK), BF16),
            pltpu.VMEM((D, TOK), F32),
            pltpu.VMEM((D, TOK), F32),
            pltpu.VMEM((2 * HEADS, TOK), F32),
            pltpu.VMEM((HEADS, TOK, TOK), BF16),
            pltpu.VMEM((D, TOK), F32),
            pltpu.VMEM((HEADS, TOK), F32),
            pltpu.VMEM((HEADS, HD + 16, TOK), BF16),
            pltpu.VMEM((3 * D, TOK), BF16),
            pltpu.VMEM((D, TOK), BF16),
        ],
        compiler_params=pltpu.CompilerParams(vmem_limit_bytes=32 * 2**20),
        cost_estimate=pl.CostEstimate(flops=2**31, bytes_accessed=2**23, transcendentals=2**20),
        name="attend",
    )(scales, mask_map, patches, cotangent, token, diag, right, below, wqkv, wproj, pbias, gain, bias)


def local(
    patches,
    cotangent,
    mask_map,
    mask_token,
    w_qkv,
    w_proj,
    proj_bias,
    norm_gain,
    scales,
    bias_table,
    rel_index,
):
    rows, cols = lax.axis_size("row"), lax.axis_size("col")
    row, col = lax.axis_index("row"), lax.axis_index("col")

    def move(block, up, left):
        pairs = [
            (((r + up) % rows) * cols + (c + left) % cols, r * cols + c)
            for r in range(rows)
            for c in range(cols)
        ]
        return lax.ppermute(block, ("row", "col"), pairs)

    diag, right, below = prep(mask_map, patches, cotangent, mask_token)
    diag = move(diag, 1, 1)
    right = move(right, 0, 1)
    below = move(below, 1, 0)

    edge = jnp.stack([row == rows - 1, col == cols - 1]).astype(jnp.int32)
    bias = build_bias(edge, rel_index, bias_table.T)
    back = attend(
        scales, mask_map, patches, cotangent, mask_token, diag, right, below, w_qkv, w_proj, proj_bias, norm_gain, bias
    )
    from_above = move(back[1], -1, 0)
    from_left = move(back[2], 0, -1)
    from_diag = move(back[3], -1, -1)
    square = lambda block: block.reshape(HALF, HALF, D)
    west = jnp.concatenate([square(from_diag), square(from_left)], axis=0)
    east = jnp.concatenate([square(from_above), square(back[0])], axis=0)
    behind = jnp.concatenate([west, east], axis=1)
    total = cotangent.astype(F32) + behind.astype(F32)
    return jnp.where((mask_map == 1)[:, :, None], 0.0, total).astype(BF16)


def solution(mesh):
    in_specs = (
        P("row", "col", None),
        P("row", "col", None),
        P("row", "col"),
        P(),
        P(),
        P(),
        P(),
        P(),
        P(),
        P(),
        P(),
    )
    return jax.shard_map(
        local, mesh=mesh, in_specs=in_specs, out_specs=P("row", "col", None), check_vma=False
    )
```

```python
import math

import jax
import jax.numpy as jnp
from jax import lax
from jax.experimental import pallas as pl
from jax.experimental.pallas import tpu as pltpu
from jax.sharding import PartitionSpec as P

WIN = 16
HALF = 8
QUART = HALF * HALF
TOK = WIN * WIN
D = 512
HEADS = 16
HD = D // HEADS
BIAS_ROWS = 961
LOG2E = math.log2(math.e)
F32 = jnp.float32
BF16 = jnp.bfloat16


def dot(a, b, ca, cb):
    return lax.dot_general(a, b, (((ca,), (cb,)), ((), ())), preferred_element_type=F32)


def hidden_at(mask_ref, r, c):
    return jnp.broadcast_to(mask_ref[r * HALF : r * HALF + 1, c * HALF : c * HALF + 1], (QUART, D)) == 1


def mixed_piece(mask_ref, patches_ref, token_ref, r, c):
    piece = patches_ref[r * HALF : (r + 1) * HALF, c * HALF : (c + 1) * HALF, :].reshape(QUART, D)
    token = jnp.broadcast_to(token_ref[...].reshape(1, D), (QUART, D))
    return jnp.where(hidden_at(mask_ref, r, c), token, piece)


def raw_piece(ref, r, c):
    return ref[r * HALF : (r + 1) * HALF, c * HALF : (c + 1) * HALF, :].reshape(QUART, D)


def prep_kernel(mask_ref, patches_ref, cot_ref, token_ref, diag_ref, right_ref, below_ref):
    for (r, c, out_ref) in ((0, 0, right_ref), (1, 0, diag_ref), (1, 1, below_ref)):
        out_ref[:QUART, :] = mixed_piece(mask_ref, patches_ref, token_ref, r, c)
        out_ref[QUART:, :] = raw_piece(cot_ref, r, c)


def prep(mask_map, patches, cotangent, token):
    vmem = pl.BlockSpec(memory_space=pltpu.VMEM)
    return pl.pallas_call(
        prep_kernel,
        out_shape=[jax.ShapeDtypeStruct((2 * QUART, D), BF16)] * 3,
        in_specs=[vmem] * 4,
        out_specs=[vmem] * 3,
        name="prep",
    )(mask_map, patches, cotangent, token)


def bias_kernel(edge_ref, facts_ref, out_ref, base):
    scaled = facts_ref[:HEADS, :] * LOG2E
    high = scaled.astype(BF16)
    table = jnp.concatenate([high, (scaled - high.astype(F32)).astype(BF16)], axis=0)
    rows = [facts_ref[i : i + 1, :TOK] for i in (16, 32, 31, 47)]
    rows = jnp.concatenate(rows * 2, axis=0).astype(jnp.int32)
    first = lax.broadcasted_iota(jnp.int32, (8, TOK), 0) < 4
    digits = jnp.where(first, rows // 8, rows % 8).astype(F32).astype(BF16)
    lane1 = lax.broadcasted_iota(jnp.int32, (1, TOK), 1)
    dr, c = lane1 // 8, lane1 % 8
    late = dr >= 15
    row = jnp.where(late, 30 - dr, 15 - dr)
    tokens = lax.broadcasted_iota(jnp.int32, (TOK, TOK), 0)
    entries = lax.broadcasted_iota(jnp.int32, (1024, TOK), 0)
    for part in range(4):
        col = (16, 8, 15, 7)[part] - c
        token = jnp.clip(row * WIN + jnp.minimum(col, 15), 0, TOK - 1)
        found = dot(digits, jnp.where(tokens == token, 1.0, 0.0).astype(BF16), 1, 0)
        pair = 2 if part >= 2 else 0
        order = found[0:4] * 8.0 + found[4:8]
        order = jnp.where(late, order[pair + 1 : pair + 2], order[pair : pair + 1]).astype(jnp.int32)
        both = dot(table, jnp.where(entries == order, 1.0, 0.0).astype(BF16), 1, 0)
        base[:, part * TOK : (part + 1) * TOK] = both[:HEADS] + both[HEADS:]

    lane = lax.broadcasted_iota(jnp.int32, (8, 256), 1)
    sub = lax.broadcasted_iota(jnp.int32, (8, 256), 0)
    straight = (lane % 8) >= sub
    lane = lax.broadcasted_iota(jnp.int32, (8, 128), 1)
    left = lane < 64
    cut = -100.0 * LOG2E
    row_cut = jnp.where(edge_ref[0] == 1, cut, 0.0)
    col_cut = jnp.where(edge_ref[1] == 1, cut, 0.0)
    masks = {}
    for ch in range(2):
        across = jnp.where(left == (ch == 0), 0.0, col_cut)
        masks[ch, 0] = across
        masks[ch, 1] = jnp.minimum(across, row_cut)

    def swap(v):
        return pltpu.roll(v, 64, 1)

    def head(h, carry):
        strips = [
            jnp.broadcast_to(base[pl.ds(h, 1), pl.ds(d * 256, 256)], (8, 256)) for d in range(4)
        ]
        here = [pltpu.roll(s, 0, 1, stride=1, stride_axis=0) for s in strips[1:]]
        wrapped = [pltpu.roll(s, 248, 1, stride=1, stride_axis=0) for s in strips[:3]]
        fields = [jnp.where(straight, a, b) for a, b in zip(here, wrapped)]
        low = [f[:, :128] for f in fields]
        top = [f[:, 128:] for f in fields]
        low_s = [swap(v) for v in low]
        top_s = [swap(v) for v in top]
        for ch in range(2):
            a, b = 1 - ch, 2 - ch
            first = [
                jnp.where(left, low[a], low_s[b]),
                jnp.where(left, low_s[a], low[b]),
                jnp.where(left, top[a], top_s[b]),
            ]
            second = [
                None,
                jnp.where(left, low_s[b], low[a]),
                jnp.where(left, top[b], top_s[a]),
                jnp.where(left, top_s[b], top[a]),
            ]
            for p in range(24):
                k, r = divmod(p, 8)
                vreg = first[k]
                if r:
                    vreg = jnp.where(lane % 64 >= 8 * r, first[k], second[k + 1])
                    vreg = pltpu.roll(vreg, 128 - 8 * r, 1)
                for rh_t in range(2):
                    for rh_s in range(2):
                        rl_s = 8 * (rh_t - rh_s) + 15 - p
                        if 0 <= rl_s < 8:
                            at = ((rh_s * 2 + ch) * 8 + rl_s) * 8
                            out_ref[h, at : at + 8, rh_t * 128 : (rh_t + 1) * 128] = (
                                vreg + masks[ch, int(rh_t != rh_s)]
                            )
        return carry

    for h in range(HEADS):
        head(h, 0)


def build_bias(edge, rel_index, table):
    slabs = [rel_index[at : at + WIN].astype(F32) for at in (0, TOK - WIN)]
    facts = jnp.concatenate(
        [jnp.pad(part, ((0, 0), (0, 1024 - part.shape[1]))) for part in (table.T, *slabs)], axis=0
    )
    vmem = pl.BlockSpec(memory_space=pltpu.VMEM)
    return pl.pallas_call(
        bias_kernel,
        out_shape=jax.ShapeDtypeStruct((HEADS, TOK, TOK), F32),
        in_specs=[pl.BlockSpec(memory_space=pltpu.SMEM), vmem],
        out_specs=vmem,
        scratch_shapes=[pltpu.VMEM((HEADS, 1024), F32)],
        compiler_params=pltpu.CompilerParams(vmem_limit_bytes=24 * 2**20),
        cost_estimate=pl.CostEstimate(flops=2**26, bytes_accessed=2**22, transcendentals=0),
        name="bias",
    )(edge, facts)


def attend_kernel(
    scales_ref, mask_ref, patches_ref, cot_ref, token_ref, diag_ref, right_ref, below_ref,
    wqkv_ref, wproj_ref, pbias_ref, gain_ref,
    bias_ref, own_out, below_out, right_out, diag_out,
    packed, qhat, khat, rnorm, weights, attended, inverse, vaug, dpacked, dattended,
):
    own = mixed_piece(mask_ref, patches_ref, token_ref, 0, 1)
    tokens = jnp.concatenate([below_ref[:QUART, :], diag_ref[:QUART, :], own, right_ref[:QUART, :]], axis=0)
    packed[...] = dot(tokens, wqkv_ref[...], 1, 0).astype(BF16).T
    ones = jnp.where(lax.broadcasted_iota(jnp.int32, (16, TOK), 0) < 2, 1.0, 0.0).astype(BF16)

    def score(h):
        rows = slice(h * HD, (h + 1) * HD)
        query = packed[h * HD : (h + 1) * HD, :].astype(F32)
        key = packed[D + h * HD : D + (h + 1) * HD, :].astype(F32)
        rq = lax.rsqrt(jnp.sum(query * query, axis=0, keepdims=True) + 1e-6)
        rk = lax.rsqrt(jnp.sum(key * key, axis=0, keepdims=True) + 1e-6)
        rnorm[h : h + 1, :] = rq
        rnorm[HEADS + h : HEADS + h + 1, :] = rk
        qn = query * rq
        kn = key * rk
        qhat[rows, :] = qn
        khat[rows, :] = kn
        return dot(kn.astype(BF16), (qn * (scales_ref[h] * LOG2E)).astype(BF16), 0, 0)

    def gather(h, raised):
        rows = slice(h * HD, (h + 1) * HD)
        vrows = jnp.concatenate([packed[2 * D + h * HD : 2 * D + (h + 1) * HD, :], ones], axis=0)
        vaug[h] = vrows
        gathered = dot(vrows, raised, 1, 0)
        inv = 1.0 / gathered[HD : HD + 1, :]
        inverse[h : h + 1, :] = inv
        attended[rows, :] = gathered[:HD] * inv

    scores, raised = {}, {}
    for step in range(HEADS + 3):
        if step < HEADS:
            scores[step] = score(step)
        h = step - 1
        if 0 <= h < HEADS:
            raised[h] = jnp.exp2(scores.pop(h) + bias_ref[h]).astype(BF16)
            weights[h] = raised[h]
        h = step - 3
        if 0 <= h < HEADS:
            gather(h, raised.pop(h))

    projected = dot(attended[...].astype(BF16), wproj_ref[...], 0, 0) + pbias_ref[...].reshape(1, D)
    centred = projected - jnp.mean(projected, axis=1, keepdims=True)
    rstd = lax.rsqrt(jnp.mean(centred * centred, axis=1, keepdims=True) + 1e-5)
    xhat = centred * rstd
    ahead = jnp.concatenate([below_ref[QUART:, :], diag_ref[QUART:, :], raw_piece(cot_ref, 0, 1), right_ref[QUART:, :]], axis=0).astype(F32)
    grad = ahead * gain_ref[...].reshape(1, D)
    grad = rstd * (
        grad
        - jnp.mean(grad, axis=1, keepdims=True)
        - xhat * jnp.mean(grad * xhat, axis=1, keepdims=True)
    )
    dattended[...] = dot(wproj_ref[...], grad.astype(BF16), 1, 1).astype(BF16)

    def spread(h):
        rows = slice(h * HD, (h + 1) * HD)
        da = dattended[rows, :]
        delta = -jnp.sum(da.astype(F32) * attended[rows, :], axis=0, keepdims=True)
        dhigh = delta.astype(BF16).astype(F32)
        tail = jnp.concatenate([dhigh, delta - dhigh, jnp.zeros((14, TOK), F32)], axis=0).astype(BF16)
        return dot(vaug[h], jnp.concatenate([da, tail], axis=0), 0, 0)

    def collect(h, dscores):
        rows = slice(h * HD, (h + 1) * HD)
        inv = inverse[h : h + 1, :]
        qn = qhat[rows, :]
        kn = khat[rows, :]
        scaled = inv * scales_ref[h]
        dv = dot((dattended[rows, :].astype(F32) * inv).astype(BF16), weights[h], 1, 1)
        dq = dot(kn.astype(BF16), dscores, 1, 0) * scaled
        dk = dot((qn * scaled).astype(BF16), dscores, 1, 1)
        return dq, dk, dv

    def finish(h, dq, dk, dv):
        rows = slice(h * HD, (h + 1) * HD)
        qn = qhat[rows, :]
        kn = khat[rows, :]
        dq = rnorm[h : h + 1, :] * (dq - qn * jnp.sum(qn * dq, axis=0, keepdims=True))
        dk = rnorm[HEADS + h : HEADS + h + 1, :] * (dk - kn * jnp.sum(kn * dk, axis=0, keepdims=True))
        dpacked[h * HD : (h + 1) * HD, :] = dq.astype(BF16)
        dpacked[D + h * HD : D + (h + 1) * HD, :] = dk.astype(BF16)
        dpacked[2 * D + h * HD : 2 * D + (h + 1) * HD, :] = dv.astype(BF16)

    dweights, dscores, grads = {}, {}, {}
    for step in range(HEADS + 3 + 1):
        if step < HEADS:
            dweights[step] = spread(step)
        h = step - 1
        if 0 <= h < HEADS:
            dscores[h] = weights[h] * dweights.pop(h).astype(BF16)
        h = step - 3
        if 0 <= h < HEADS:
            grads[h] = collect(h, dscores.pop(h))
        h = step - 3 - 1
        if 0 <= h < HEADS:
            finish(h, *grads.pop(h))

    result = dot(wqkv_ref[...], dpacked[...], 1, 0).astype(BF16).T
    for i, ref in enumerate((below_out, diag_out, own_out, right_out)):
        ref[...] = result[i * QUART : (i + 1) * QUART, :]


def attend(scales, mask_map, patches, cotangent, token, diag, right, below, wqkv, wproj, pbias, gain, bias):
    vmem = pl.BlockSpec(memory_space=pltpu.VMEM)
    return pl.pallas_call(
        attend_kernel,
        out_shape=[jax.ShapeDtypeStruct((QUART, D), BF16)] * 4,
        in_specs=[pl.BlockSpec(memory_space=pltpu.SMEM)] + [vmem] * 12,
        out_specs=[vmem] * 4,
        scratch_shapes=[
            pltpu.VMEM((3 * D, TOK), BF16),
            pltpu.VMEM((D, TOK), F32),
            pltpu.VMEM((D, TOK), F32),
            pltpu.VMEM((2 * HEADS, TOK), F32),
            pltpu.VMEM((HEADS, TOK, TOK), BF16),
            pltpu.VMEM((D, TOK), F32),
            pltpu.VMEM((HEADS, TOK), F32),
            pltpu.VMEM((HEADS, HD + 16, TOK), BF16),
            pltpu.VMEM((3 * D, TOK), BF16),
            pltpu.VMEM((D, TOK), BF16),
        ],
        compiler_params=pltpu.CompilerParams(vmem_limit_bytes=32 * 2**20),
        cost_estimate=pl.CostEstimate(flops=2**31, bytes_accessed=2**23, transcendentals=2**20),
        name="attend",
    )(scales, mask_map, patches, cotangent, token, diag, right, below, wqkv, wproj, pbias, gain, bias)


def local(
    patches,
    cotangent,
    mask_map,
    mask_token,
    w_qkv,
    w_proj,
    proj_bias,
    norm_gain,
    scales,
    bias_table,
    rel_index,
):
    rows, cols = lax.axis_size("row"), lax.axis_size("col")
    row, col = lax.axis_index("row"), lax.axis_index("col")

    def move(block, up, left):
        pairs = [
            (((r + up) % rows) * cols + (c + left) % cols, r * cols + c)
            for r in range(rows)
            for c in range(cols)
        ]
        return lax.ppermute(block, ("row", "col"), pairs)

    diag, right, below = prep(mask_map, patches, cotangent, mask_token)
    diag = move(diag, -1, 1)
    right = move(right, 0, 1)
    below = move(below, -1, 0)

    edge = jnp.stack([row == 0, col == cols - 1]).astype(jnp.int32)
    bias = build_bias(edge, rel_index, bias_table)
    back = attend(
        scales, mask_map, patches, cotangent, mask_token, diag, right, below, w_qkv, w_proj, proj_bias, norm_gain, bias
    )
    from_above = move(back[1], 1, 0)
    from_left = move(back[2], 0, -1)
    from_diag = move(back[3], 1, -1)
    square = lambda block: block.reshape(HALF, HALF, D)
    def placed(block, r, c):
        return jnp.pad(square(block), ((r * HALF, HALF - r * HALF), (c * HALF, HALF - c * HALF), (0, 0)))

    behind = placed(from_diag, 1, 0) + placed(from_left, 0, 0) + placed(from_above, 1, 1) + placed(back[0], 0, 1)
    total = cotangent.astype(F32) + behind.astype(F32)
    return jnp.where((mask_map == 1)[:, :, None], 0.0, total).astype(BF16)


def solution(mesh):
    in_specs = (
        P("row", "col", None),
        P("row", "col", None),
        P("row", "col"),
        P(),
        P(),
        P(),
        P(),
        P(),
        P(),
        P(),
        P(),
    )
    return jax.shard_map(
        local, mesh=mesh, in_specs=in_specs, out_specs=P("row", "col", None), check_vma=False
    )
```

```python
import math

import jax
import jax.numpy as jnp
from jax import lax
from jax.experimental import pallas as pl
from jax.experimental.pallas import tpu as pltpu
from jax.sharding import PartitionSpec as P

WIN = 16
HALF = 8
QUART = HALF * HALF
TOK = WIN * WIN
D = 512
HEADS = 16
HD = D // HEADS
BIAS_ROWS = 961
LOG2E = math.log2(math.e)
F32 = jnp.float32
BF16 = jnp.bfloat16


def dot(a, b, ca, cb):
    return lax.dot_general(a, b, (((ca,), (cb,)), ((), ())), preferred_element_type=F32)


def hidden_at(mask_ref, r, c):
    return jnp.broadcast_to(mask_ref[r * HALF : r * HALF + 1, c * HALF : c * HALF + 1], (QUART, D)) == 1


def mixed_piece(mask_ref, patches_ref, token_ref, r, c):
    piece = patches_ref[r * HALF : (r + 1) * HALF, c * HALF : (c + 1) * HALF, :].reshape(QUART, D)
    token = jnp.broadcast_to(token_ref[...].reshape(1, D), (QUART, D))
    return jnp.where(hidden_at(mask_ref, r, c), token, piece)


def raw_piece(ref, r, c):
    return ref[r * HALF : (r + 1) * HALF, c * HALF : (c + 1) * HALF, :].reshape(QUART, D)


def prep_kernel(mask_ref, patches_ref, cot_ref, token_ref, diag_ref, right_ref, below_ref):
    for (r, c, out_ref) in ((0, 0, right_ref), (1, 0, diag_ref), (1, 1, below_ref)):
        out_ref[:QUART, :] = mixed_piece(mask_ref, patches_ref, token_ref, r, c)
        out_ref[QUART:, :] = raw_piece(cot_ref, r, c)


def prep(mask_map, patches, cotangent, token):
    vmem = pl.BlockSpec(memory_space=pltpu.VMEM)
    return pl.pallas_call(
        prep_kernel,
        out_shape=[pltpu.VMEM((2 * QUART, D), BF16)] * 3,
        in_specs=[vmem] * 4,
        out_specs=[vmem] * 3,
        name="prep",
    )(mask_map, patches, cotangent, token)


def bias_kernel(edge_ref, facts_ref, out_ref, base):
    scaled = facts_ref[:HEADS, :] * LOG2E
    high = scaled.astype(BF16)
    table = jnp.concatenate([high, (scaled - high.astype(F32)).astype(BF16)], axis=0)
    rows = [facts_ref[i : i + 1, :TOK] for i in (16, 32, 31, 47)]
    rows = jnp.concatenate(rows * 2, axis=0).astype(jnp.int32)
    first = lax.broadcasted_iota(jnp.int32, (8, TOK), 0) < 4
    digits = jnp.where(first, rows // 8, rows % 8).astype(F32).astype(BF16)
    lane1 = lax.broadcasted_iota(jnp.int32, (1, TOK), 1)
    dr, c = lane1 // 8, lane1 % 8
    late = dr >= 15
    row = jnp.where(late, 30 - dr, 15 - dr)
    tokens = lax.broadcasted_iota(jnp.int32, (TOK, TOK), 0)
    entries = lax.broadcasted_iota(jnp.int32, (1024, TOK), 0)
    for part in range(4):
        col = (16, 8, 15, 7)[part] - c
        token = jnp.clip(row * WIN + jnp.minimum(col, 15), 0, TOK - 1)
        found = dot(digits, jnp.where(tokens == token, 1.0, 0.0).astype(BF16), 1, 0)
        pair = 2 if part >= 2 else 0
        order = found[0:4] * 8.0 + found[4:8]
        order = jnp.where(late, order[pair + 1 : pair + 2], order[pair : pair + 1]).astype(jnp.int32)
        both = dot(table, jnp.where(entries == order, 1.0, 0.0).astype(BF16), 1, 0)
        base[:, part * TOK : (part + 1) * TOK] = both[:HEADS] + both[HEADS:]

    lane = lax.broadcasted_iota(jnp.int32, (8, 256), 1)
    sub = lax.broadcasted_iota(jnp.int32, (8, 256), 0)
    straight = (lane % 8) >= sub
    lane = lax.broadcasted_iota(jnp.int32, (8, 128), 1)
    left = lane < 64
    cut = -100.0 * LOG2E
    row_cut = jnp.where(edge_ref[0] == 1, cut, 0.0)
    col_cut = jnp.where(edge_ref[1] == 1, cut, 0.0)
    masks = {}
    for ch in range(2):
        across = jnp.where(left == (ch == 0), 0.0, col_cut)
        masks[ch, 0] = across
        masks[ch, 1] = jnp.minimum(across, row_cut)

    def swap(v):
        return pltpu.roll(v, 64, 1)

    def head(h, carry):
        strips = [
            jnp.broadcast_to(base[pl.ds(h, 1), pl.ds(d * 256, 256)], (8, 256)) for d in range(4)
        ]
        here = [pltpu.roll(s, 0, 1, stride=1, stride_axis=0) for s in strips[1:]]
        wrapped = [pltpu.roll(s, 248, 1, stride=1, stride_axis=0) for s in strips[:3]]
        fields = [jnp.where(straight, a, b) for a, b in zip(here, wrapped)]
        low = [f[:, :128] for f in fields]
        top = [f[:, 128:] for f in fields]
        low_s = [swap(v) for v in low]
        top_s = [swap(v) for v in top]
        for ch in range(2):
            a, b = 1 - ch, 2 - ch
            first = [
                jnp.where(left, low[a], low_s[b]),
                jnp.where(left, low_s[a], low[b]),
                jnp.where(left, top[a], top_s[b]),
            ]
            second = [
                None,
                jnp.where(left, low_s[b], low[a]),
                jnp.where(left, top[b], top_s[a]),
                jnp.where(left, top_s[b], top[a]),
            ]
            for p in range(24):
                k, r = divmod(p, 8)
                vreg = first[k]
                if r:
                    vreg = jnp.where(lane % 64 >= 8 * r, first[k], second[k + 1])
                    vreg = pltpu.roll(vreg, 128 - 8 * r, 1)
                for rh_t in range(2):
                    for rh_s in range(2):
                        rl_s = 8 * (rh_t - rh_s) + 15 - p
                        if 0 <= rl_s < 8:
                            at = ((rh_s * 2 + ch) * 8 + rl_s) * 8
                            out_ref[h, at : at + 8, rh_t * 128 : (rh_t + 1) * 128] = (
                                vreg + masks[ch, int(rh_t != rh_s)]
                            )
        return carry

    for h in range(HEADS):
        head(h, 0)


def build_bias(edge, rel_index, table):
    slabs = [rel_index[at : at + WIN].astype(F32) for at in (0, TOK - WIN)]
    facts = jnp.concatenate(
        [jnp.pad(part, ((0, 0), (0, 1024 - part.shape[1]))) for part in (table.T, *slabs)], axis=0
    )
    vmem = pl.BlockSpec(memory_space=pltpu.VMEM)
    return pl.pallas_call(
        bias_kernel,
        out_shape=jax.ShapeDtypeStruct((HEADS, TOK, TOK), F32),
        in_specs=[pl.BlockSpec(memory_space=pltpu.SMEM), vmem],
        out_specs=vmem,
        scratch_shapes=[pltpu.VMEM((HEADS, 1024), F32)],
        compiler_params=pltpu.CompilerParams(vmem_limit_bytes=24 * 2**20),
        cost_estimate=pl.CostEstimate(flops=2**26, bytes_accessed=2**22, transcendentals=0),
        name="bias",
    )(edge, facts)


def attend_kernel(
    scales_ref, mask_ref, patches_ref, cot_ref, token_ref, diag_ref, right_ref, below_ref,
    wqkv_ref, wproj_ref, pbias_ref, gain_ref,
    bias_ref, own_out, below_out, right_out, diag_out,
    packed, qhat, khat, rnorm, weights, attended, inverse, vaug, dpacked, dattended,
):
    own = mixed_piece(mask_ref, patches_ref, token_ref, 0, 1)
    tokens = jnp.concatenate([below_ref[:QUART, :], diag_ref[:QUART, :], own, right_ref[:QUART, :]], axis=0)

    def project(half):
        for part in range(3):
            at = slice(part * D + half * D // 2, part * D + (half + 1) * D // 2)
            packed[at, :] = dot(tokens, wqkv_ref[:, at], 1, 0).astype(BF16).T

    project(0)
    ones = jnp.where(lax.broadcasted_iota(jnp.int32, (16, TOK), 0) < 2, 1.0, 0.0).astype(BF16)

    def score(h):
        rows = slice(h * HD, (h + 1) * HD)
        query = packed[h * HD : (h + 1) * HD, :].astype(F32)
        key = packed[D + h * HD : D + (h + 1) * HD, :].astype(F32)
        rq = lax.rsqrt(jnp.sum(query * query, axis=0, keepdims=True) + 1e-6)
        rk = lax.rsqrt(jnp.sum(key * key, axis=0, keepdims=True) + 1e-6)
        rnorm[h : h + 1, :] = rq
        rnorm[HEADS + h : HEADS + h + 1, :] = rk
        qn = query * rq
        kn = key * rk
        qhat[rows, :] = qn
        khat[rows, :] = kn
        return dot(kn.astype(BF16), (qn * (scales_ref[h] * LOG2E)).astype(BF16), 0, 0)

    def gather(h, raised):
        rows = slice(h * HD, (h + 1) * HD)
        vrows = jnp.concatenate([packed[2 * D + h * HD : 2 * D + (h + 1) * HD, :], ones], axis=0)
        vaug[h] = vrows
        gathered = dot(vrows, raised, 1, 0)
        inv = 1.0 / gathered[HD : HD + 1, :]
        inverse[h : h + 1, :] = inv
        attended[rows, :] = gathered[:HD] * inv

    scores, raised = {}, {}
    for step in range(HEADS + 3):
        if step == 4:
            project(1)
        if step < HEADS:
            scores[step] = score(step)
        h = step - 1
        if 0 <= h < HEADS:
            raised[h] = jnp.exp2(scores.pop(h) + bias_ref[h]).astype(BF16)
            weights[h] = raised[h]
        h = step - 3
        if 0 <= h < HEADS:
            gather(h, raised.pop(h))

    projected = dot(attended[...].astype(BF16), wproj_ref[...], 0, 0) + pbias_ref[...].reshape(1, D)
    centred = projected - jnp.mean(projected, axis=1, keepdims=True)
    rstd = lax.rsqrt(jnp.mean(centred * centred, axis=1, keepdims=True) + 1e-5)
    xhat = centred * rstd
    ahead = jnp.concatenate([below_ref[QUART:, :], diag_ref[QUART:, :], raw_piece(cot_ref, 0, 1), right_ref[QUART:, :]], axis=0).astype(F32)
    grad = ahead * gain_ref[...].reshape(1, D)
    grad = rstd * (
        grad
        - jnp.mean(grad, axis=1, keepdims=True)
        - xhat * jnp.mean(grad * xhat, axis=1, keepdims=True)
    )
    dattended[...] = dot(wproj_ref[...], grad.astype(BF16), 1, 1).astype(BF16)

    def spread(h):
        rows = slice(h * HD, (h + 1) * HD)
        da = dattended[rows, :]
        delta = -jnp.sum(da.astype(F32) * attended[rows, :], axis=0, keepdims=True)
        dhigh = delta.astype(BF16).astype(F32)
        tail = jnp.concatenate([dhigh, delta - dhigh, jnp.zeros((14, TOK), F32)], axis=0).astype(BF16)
        return dot(vaug[h], jnp.concatenate([da, tail], axis=0), 0, 0)

    def collect(h, dscores):
        rows = slice(h * HD, (h + 1) * HD)
        inv = inverse[h : h + 1, :]
        qn = qhat[rows, :]
        kn = khat[rows, :]
        scaled = inv * scales_ref[h]
        dv = dot((dattended[rows, :].astype(F32) * inv).astype(BF16), weights[h], 1, 1)
        dq = dot(kn.astype(BF16), dscores, 1, 0) * scaled
        dk = dot((qn * scaled).astype(BF16), dscores, 1, 1)
        return dq, dk, dv

    def finish(h, dq, dk, dv):
        rows = slice(h * HD, (h + 1) * HD)
        qn = qhat[rows, :]
        kn = khat[rows, :]
        dq = rnorm[h : h + 1, :] * (dq - qn * jnp.sum(qn * dq, axis=0, keepdims=True))
        dk = rnorm[HEADS + h : HEADS + h + 1, :] * (dk - kn * jnp.sum(kn * dk, axis=0, keepdims=True))
        dpacked[h * HD : (h + 1) * HD, :] = dq.astype(BF16)
        dpacked[D + h * HD : D + (h + 1) * HD, :] = dk.astype(BF16)
        dpacked[2 * D + h * HD : 2 * D + (h + 1) * HD, :] = dv.astype(BF16)

    dweights, dscores, grads = {}, {}, {}
    for step in range(HEADS + 3 + 1):
        if step < HEADS:
            dweights[step] = spread(step)
        h = step - 1
        if 0 <= h < HEADS:
            dscores[h] = weights[h] * dweights.pop(h).astype(BF16)
        h = step - 3
        if 0 <= h < HEADS:
            grads[h] = collect(h, dscores.pop(h))
        h = step - 3 - 1
        if 0 <= h < HEADS:
            finish(h, *grads.pop(h))

    result = dot(wqkv_ref[...], dpacked[...], 1, 0).astype(BF16).T
    for i, ref in enumerate((below_out, diag_out, own_out, right_out)):
        ref[...] = result[i * QUART : (i + 1) * QUART, :]


def attend(scales, mask_map, patches, cotangent, token, diag, right, below, wqkv, wproj, pbias, gain, bias):
    vmem = pl.BlockSpec(memory_space=pltpu.VMEM)
    return pl.pallas_call(
        attend_kernel,
        out_shape=[jax.ShapeDtypeStruct((QUART, D), BF16)] * 4,
        in_specs=[pl.BlockSpec(memory_space=pltpu.SMEM)] + [vmem] * 12,
        out_specs=[vmem] * 4,
        scratch_shapes=[
            pltpu.VMEM((3 * D, TOK), BF16),
            pltpu.VMEM((D, TOK), F32),
            pltpu.VMEM((D, TOK), F32),
            pltpu.VMEM((2 * HEADS, TOK), F32),
            pltpu.VMEM((HEADS, TOK, TOK), BF16),
            pltpu.VMEM((D, TOK), F32),
            pltpu.VMEM((HEADS, TOK), F32),
            pltpu.VMEM((HEADS, HD + 16, TOK), BF16),
            pltpu.VMEM((3 * D, TOK), BF16),
            pltpu.VMEM((D, TOK), BF16),
        ],
        compiler_params=pltpu.CompilerParams(vmem_limit_bytes=32 * 2**20),
        cost_estimate=pl.CostEstimate(flops=2**31, bytes_accessed=2**23, transcendentals=2**20),
        name="attend",
    )(scales, mask_map, patches, cotangent, token, diag, right, below, wqkv, wproj, pbias, gain, bias)


def local(
    patches,
    cotangent,
    mask_map,
    mask_token,
    w_qkv,
    w_proj,
    proj_bias,
    norm_gain,
    scales,
    bias_table,
    rel_index,
):
    rows, cols = lax.axis_size("row"), lax.axis_size("col")
    row, col = lax.axis_index("row"), lax.axis_index("col")

    def move(block, up, left):
        pairs = [
            (((r + up) % rows) * cols + (c + left) % cols, r * cols + c)
            for r in range(rows)
            for c in range(cols)
        ]
        return lax.ppermute(block, ("row", "col"), pairs)

    diag, right, below = prep(mask_map, patches, cotangent, mask_token)
    diag = move(diag, -1, 1)
    right = move(right, 0, 1)
    below = move(below, -1, 0)

    edge = jnp.stack([row == 0, col == cols - 1]).astype(jnp.int32)
    bias = build_bias(edge, rel_index, bias_table)
    back = attend(
        scales, mask_map, patches, cotangent, mask_token, diag, right, below, w_qkv, w_proj, proj_bias, norm_gain, bias
    )
    from_above = move(back[1], 1, 0)
    from_left = move(back[2], 0, -1)
    from_diag = move(back[3], 1, -1)
    square = lambda block: block.reshape(HALF, HALF, D)
    def placed(block, r, c):
        return jnp.pad(square(block), ((r * HALF, HALF - r * HALF), (c * HALF, HALF - c * HALF), (0, 0)))

    behind = placed(from_diag, 1, 0) + placed(from_left, 0, 0) + placed(from_above, 1, 1) + placed(back[0], 0, 1)
    total = cotangent.astype(F32) + behind.astype(F32)
    return jnp.where((mask_map == 1)[:, :, None], 0.0, total).astype(BF16)


def solution(mesh):
    in_specs = (
        P("row", "col", None),
        P("row", "col", None),
        P("row", "col"),
        P(),
        P(),
        P(),
        P(),
        P(),
        P(),
        P(),
        P(),
    )
    return jax.shard_map(
        local, mesh=mesh, in_specs=in_specs, out_specs=P("row", "col", None), check_vma=False
    )
```

```python
import math

import jax
import jax.numpy as jnp
from jax import lax
from jax.experimental import pallas as pl
from jax.experimental.pallas import tpu as pltpu
from jax.sharding import PartitionSpec as P

WIN = 16
HALF = 8
QUART = HALF * HALF
TOK = WIN * WIN
D = 512
HEADS = 16
HD = D // HEADS
BIAS_ROWS = 961
LOG2E = math.log2(math.e)
F32 = jnp.float32
BF16 = jnp.bfloat16


def dot(a, b, ca, cb):
    return lax.dot_general(a, b, (((ca,), (cb,)), ((), ())), preferred_element_type=F32)


def hidden_at(mask_ref, r, c):
    return jnp.broadcast_to(mask_ref[r * HALF : r * HALF + 1, c * HALF : c * HALF + 1], (QUART, D)) == 1


def mixed_piece(mask_ref, patches_ref, token_ref, r, c):
    piece = patches_ref[r * HALF : (r + 1) * HALF, c * HALF : (c + 1) * HALF, :].reshape(QUART, D)
    token = jnp.broadcast_to(token_ref[...].reshape(1, D), (QUART, D))
    return jnp.where(hidden_at(mask_ref, r, c), token, piece)


def raw_piece(ref, r, c):
    return ref[r * HALF : (r + 1) * HALF, c * HALF : (c + 1) * HALF, :].reshape(QUART, D)


def prep_kernel(mask_ref, patches_ref, cot_ref, token_ref, diag_ref, right_ref, below_ref):
    for (r, c, out_ref) in ((0, 0, right_ref), (1, 0, diag_ref), (1, 1, below_ref)):
        out_ref[:QUART, :] = mixed_piece(mask_ref, patches_ref, token_ref, r, c)
        out_ref[QUART:, :] = raw_piece(cot_ref, r, c)


def prep(mask_map, patches, cotangent, token):
    vmem = pl.BlockSpec(memory_space=pltpu.VMEM)
    return pl.pallas_call(
        prep_kernel,
        out_shape=[pltpu.VMEM((2 * QUART, D), BF16)] * 3,
        in_specs=[vmem] * 4,
        out_specs=[vmem] * 3,
        name="prep",
    )(mask_map, patches, cotangent, token)


def bias_kernel(edge_ref, facts_ref, out_ref, base):
    scaled = facts_ref[:HEADS, :] * LOG2E
    high = scaled.astype(BF16)
    table = jnp.concatenate([high, (scaled - high.astype(F32)).astype(BF16)], axis=0)
    rows = [facts_ref[i : i + 1, :TOK] for i in (16, 32, 31, 47)]
    rows = jnp.concatenate(rows * 2, axis=0).astype(jnp.int32)
    first = lax.broadcasted_iota(jnp.int32, (8, TOK), 0) < 4
    digits = jnp.where(first, rows // 8, rows % 8).astype(F32).astype(BF16)
    lane1 = lax.broadcasted_iota(jnp.int32, (1, TOK), 1)
    dr, c = lane1 // 8, lane1 % 8
    late = dr >= 15
    row = jnp.where(late, 30 - dr, 15 - dr)
    tokens = lax.broadcasted_iota(jnp.int32, (TOK, TOK), 0)
    entries = lax.broadcasted_iota(jnp.int32, (1024, TOK), 0)
    for part in range(4):
        col = (16, 8, 15, 7)[part] - c
        token = jnp.clip(row * WIN + jnp.minimum(col, 15), 0, TOK - 1)
        found = dot(digits, jnp.where(tokens == token, 1.0, 0.0).astype(BF16), 1, 0)
        pair = 2 if part >= 2 else 0
        order = found[0:4] * 8.0 + found[4:8]
        order = jnp.where(late, order[pair + 1 : pair + 2], order[pair : pair + 1]).astype(jnp.int32)
        both = dot(table, jnp.where(entries == order, 1.0, 0.0).astype(BF16), 1, 0)
        base[:, part * TOK : (part + 1) * TOK] = both[:HEADS] + both[HEADS:]

    lane = lax.broadcasted_iota(jnp.int32, (8, 256), 1)
    sub = lax.broadcasted_iota(jnp.int32, (8, 256), 0)
    straight = (lane % 8) >= sub
    lane = lax.broadcasted_iota(jnp.int32, (8, 128), 1)
    left = lane < 64
    cut = -100.0 * LOG2E
    row_cut = jnp.where(edge_ref[0] == 1, cut, 0.0)
    col_cut = jnp.where(edge_ref[1] == 1, cut, 0.0)
    masks = {}
    for ch in range(2):
        across = jnp.where(left == (ch == 0), 0.0, col_cut)
        masks[ch, 0] = across
        masks[ch, 1] = jnp.minimum(across, row_cut)

    def swap(v):
        return pltpu.roll(v, 64, 1)

    def head(h, carry):
        strips = [
            jnp.broadcast_to(base[pl.ds(h, 1), pl.ds(d * 256, 256)], (8, 256)) for d in range(4)
        ]
        here = [pltpu.roll(s, 0, 1, stride=1, stride_axis=0) for s in strips[1:]]
        wrapped = [pltpu.roll(s, 248, 1, stride=1, stride_axis=0) for s in strips[:3]]
        fields = [jnp.where(straight, a, b) for a, b in zip(here, wrapped)]
        low = [f[:, :128] for f in fields]
        top = [f[:, 128:] for f in fields]
        low_s = [swap(v) for v in low]
        top_s = [swap(v) for v in top]
        for ch in range(2):
            a, b = 1 - ch, 2 - ch
            first = [
                jnp.where(left, low[a], low_s[b]),
                jnp.where(left, low_s[a], low[b]),
                jnp.where(left, top[a], top_s[b]),
            ]
            second = [
                None,
                jnp.where(left, low_s[b], low[a]),
                jnp.where(left, top[b], top_s[a]),
                jnp.where(left, top_s[b], top[a]),
            ]
            for p in range(24):
                k, r = divmod(p, 8)
                vreg = first[k]
                if r:
                    vreg = jnp.where(lane % 64 >= 8 * r, first[k], second[k + 1])
                    vreg = pltpu.roll(vreg, 128 - 8 * r, 1)
                for rh_t in range(2):
                    for rh_s in range(2):
                        rl_s = 8 * (rh_t - rh_s) + 15 - p
                        if 0 <= rl_s < 8:
                            at = ((rh_s * 2 + ch) * 8 + rl_s) * 8
                            out_ref[h, at : at + 8, rh_t * 128 : (rh_t + 1) * 128] = (
                                vreg + masks[ch, int(rh_t != rh_s)]
                            )
        return carry

    for h in range(HEADS):
        head(h, 0)


def build_bias(edge, rel_index, table):
    slabs = [rel_index[at : at + WIN].astype(F32) for at in (0, TOK - WIN)]
    facts = jnp.concatenate(
        [jnp.pad(part, ((0, 0), (0, 1024 - part.shape[1]))) for part in (table.T, *slabs)], axis=0
    )
    vmem = pl.BlockSpec(memory_space=pltpu.VMEM)
    return pl.pallas_call(
        bias_kernel,
        out_shape=jax.ShapeDtypeStruct((HEADS, TOK, TOK), F32),
        in_specs=[pl.BlockSpec(memory_space=pltpu.SMEM), vmem],
        out_specs=vmem,
        scratch_shapes=[pltpu.VMEM((HEADS, 1024), F32)],
        compiler_params=pltpu.CompilerParams(vmem_limit_bytes=24 * 2**20),
        cost_estimate=pl.CostEstimate(flops=2**26, bytes_accessed=2**22, transcendentals=0),
        name="bias",
    )(edge, facts)


def attend_kernel(
    scales_ref, mask_ref, patches_ref, cot_ref, token_ref, diag_ref, right_ref, below_ref,
    wqkv_ref, wproj_ref, pbias_ref, gain_ref,
    bias_ref, own_out, below_out, right_out, diag_out,
    packed, qhat, khat, rnorm, weights, attended, inverse, vaug, dpacked, dattended,
):
    own = mixed_piece(mask_ref, patches_ref, token_ref, 0, 1)
    tokens = jnp.concatenate([below_ref[:QUART, :], diag_ref[:QUART, :], own, right_ref[:QUART, :]], axis=0)

    def project(half):
        for part in range(3):
            at = slice(part * D + half * D // 2, part * D + (half + 1) * D // 2)
            packed[at, :] = dot(tokens, wqkv_ref[:, at], 1, 0).astype(BF16).T

    project(0)
    ones = jnp.where(lax.broadcasted_iota(jnp.int32, (16, TOK), 0) < 2, 1.0, 0.0).astype(BF16)

    def score(h):
        rows = slice(h * HD, (h + 1) * HD)
        query = packed[h * HD : (h + 1) * HD, :].astype(F32)
        key = packed[D + h * HD : D + (h + 1) * HD, :].astype(F32)
        rq = lax.rsqrt(jnp.sum(query * query, axis=0, keepdims=True) + 1e-6)
        rk = lax.rsqrt(jnp.sum(key * key, axis=0, keepdims=True) + 1e-6)
        rnorm[h : h + 1, :] = rq
        rnorm[HEADS + h : HEADS + h + 1, :] = rk
        qn = query * rq
        kn = key * rk
        qhat[rows, :] = qn
        khat[rows, :] = kn
        return dot(kn.astype(BF16), (qn * (scales_ref[h] * LOG2E)).astype(BF16), 0, 0)

    def gather(h, raised):
        rows = slice(h * HD, (h + 1) * HD)
        vrows = jnp.concatenate([packed[2 * D + h * HD : 2 * D + (h + 1) * HD, :], ones], axis=0)
        vaug[h] = vrows
        gathered = dot(vrows, raised, 1, 0)
        inv = 1.0 / gathered[HD : HD + 1, :]
        inverse[h : h + 1, :] = inv
        attended[rows, :] = gathered[:HD] * inv

    scores, raised = {}, {}
    for step in range(HEADS + 5):
        if step == 3:
            project(1)
        if step < HEADS:
            scores[step] = score(step)
        h = step - 2
        if 0 <= h < HEADS:
            raised[h] = jnp.exp2(scores.pop(h) + bias_ref[h]).astype(BF16)
            weights[h] = raised[h]
        h = step - 5
        if 0 <= h < HEADS:
            gather(h, raised.pop(h))

    projected = dot(attended[...].astype(BF16), wproj_ref[...], 0, 0) + pbias_ref[...].reshape(1, D)
    centred = projected - jnp.mean(projected, axis=1, keepdims=True)
    rstd = lax.rsqrt(jnp.mean(centred * centred, axis=1, keepdims=True) + 1e-5)
    xhat = centred * rstd
    ahead = jnp.concatenate([below_ref[QUART:, :], diag_ref[QUART:, :], raw_piece(cot_ref, 0, 1), right_ref[QUART:, :]], axis=0).astype(F32)
    grad = ahead * gain_ref[...].reshape(1, D)
    grad = rstd * (
        grad
        - jnp.mean(grad, axis=1, keepdims=True)
        - xhat * jnp.mean(grad * xhat, axis=1, keepdims=True)
    )
    dattended[...] = dot(wproj_ref[...], grad.astype(BF16), 1, 1).astype(BF16)

    def spread(h):
        rows = slice(h * HD, (h + 1) * HD)
        da = dattended[rows, :]
        delta = -jnp.sum(da.astype(F32) * attended[rows, :], axis=0, keepdims=True)
        dhigh = delta.astype(BF16).astype(F32)
        tail = jnp.concatenate([dhigh, delta - dhigh, jnp.zeros((14, TOK), F32)], axis=0).astype(BF16)
        return dot(vaug[h], jnp.concatenate([da, tail], axis=0), 0, 0)

    def collect(h, dscores):
        rows = slice(h * HD, (h + 1) * HD)
        inv = inverse[h : h + 1, :]
        qn = qhat[rows, :]
        kn = khat[rows, :]
        scaled = inv * scales_ref[h]
        dv = dot((dattended[rows, :].astype(F32) * inv).astype(BF16), weights[h], 1, 1)
        dq = dot(kn.astype(BF16), dscores, 1, 0) * scaled
        dk = dot((qn * scaled).astype(BF16), dscores, 1, 1)
        return dq, dk, dv

    def finish(h, dq, dk, dv):
        rows = slice(h * HD, (h + 1) * HD)
        qn = qhat[rows, :]
        kn = khat[rows, :]
        dq = rnorm[h : h + 1, :] * (dq - qn * jnp.sum(qn * dq, axis=0, keepdims=True))
        dk = rnorm[HEADS + h : HEADS + h + 1, :] * (dk - kn * jnp.sum(kn * dk, axis=0, keepdims=True))
        dpacked[h * HD : (h + 1) * HD, :] = dq.astype(BF16)
        dpacked[D + h * HD : D + (h + 1) * HD, :] = dk.astype(BF16)
        dpacked[2 * D + h * HD : 2 * D + (h + 1) * HD, :] = dv.astype(BF16)

    dweights, dscores, grads = {}, {}, {}
    for step in range(HEADS + 3 + 1):
        if step < HEADS:
            dweights[step] = spread(step)
        h = step - 2
        if 0 <= h < HEADS:
            dscores[h] = weights[h] * dweights.pop(h).astype(BF16)
        h = step - 3
        if 0 <= h < HEADS:
            grads[h] = collect(h, dscores.pop(h))
        h = step - 3 - 1
        if 0 <= h < HEADS:
            finish(h, *grads.pop(h))

    result = dot(wqkv_ref[...], dpacked[...], 1, 0).astype(BF16).T
    for i, ref in enumerate((below_out, diag_out, own_out, right_out)):
        ref[...] = result[i * QUART : (i + 1) * QUART, :]


def attend(scales, mask_map, patches, cotangent, token, diag, right, below, wqkv, wproj, pbias, gain, bias):
    vmem = pl.BlockSpec(memory_space=pltpu.VMEM)
    return pl.pallas_call(
        attend_kernel,
        out_shape=[jax.ShapeDtypeStruct((QUART, D), BF16)] * 4,
        in_specs=[pl.BlockSpec(memory_space=pltpu.SMEM)] + [vmem] * 12,
        out_specs=[vmem] * 4,
        scratch_shapes=[
            pltpu.VMEM((3 * D, TOK), BF16),
            pltpu.VMEM((D, TOK), F32),
            pltpu.VMEM((D, TOK), F32),
            pltpu.VMEM((2 * HEADS, TOK), F32),
            pltpu.VMEM((HEADS, TOK, TOK), BF16),
            pltpu.VMEM((D, TOK), F32),
            pltpu.VMEM((HEADS, TOK), F32),
            pltpu.VMEM((HEADS, HD + 16, TOK), BF16),
            pltpu.VMEM((3 * D, TOK), BF16),
            pltpu.VMEM((D, TOK), BF16),
        ],
        compiler_params=pltpu.CompilerParams(vmem_limit_bytes=32 * 2**20),
        cost_estimate=pl.CostEstimate(flops=2**31, bytes_accessed=2**23, transcendentals=2**20),
        name="attend",
    )(scales, mask_map, patches, cotangent, token, diag, right, below, wqkv, wproj, pbias, gain, bias)


def local(
    patches,
    cotangent,
    mask_map,
    mask_token,
    w_qkv,
    w_proj,
    proj_bias,
    norm_gain,
    scales,
    bias_table,
    rel_index,
):
    rows, cols = lax.axis_size("row"), lax.axis_size("col")
    row, col = lax.axis_index("row"), lax.axis_index("col")

    def move(block, up, left):
        pairs = [
            (((r + up) % rows) * cols + (c + left) % cols, r * cols + c)
            for r in range(rows)
            for c in range(cols)
        ]
        return lax.ppermute(block, ("row", "col"), pairs)

    diag, right, below = prep(mask_map, patches, cotangent, mask_token)
    diag = move(diag, -1, 1)
    right = move(right, 0, 1)
    below = move(below, -1, 0)

    edge = jnp.stack([row == 0, col == cols - 1]).astype(jnp.int32)
    bias = build_bias(edge, rel_index, bias_table)
    back = attend(
        scales, mask_map, patches, cotangent, mask_token, diag, right, below, w_qkv, w_proj, proj_bias, norm_gain, bias
    )
    from_above = move(back[1], 1, 0)
    from_left = move(back[2], 0, -1)
    from_diag = move(back[3], 1, -1)
    square = lambda block: block.reshape(HALF, HALF, D)
    def placed(block, r, c):
        return jnp.pad(square(block), ((r * HALF, HALF - r * HALF), (c * HALF, HALF - c * HALF), (0, 0)))

    behind = placed(from_diag, 1, 0) + placed(from_left, 0, 0) + placed(from_above, 1, 1) + placed(back[0], 0, 1)
    total = cotangent.astype(F32) + behind.astype(F32)
    return jnp.where((mask_map == 1)[:, :, None], 0.0, total).astype(BF16)


def solution(mesh):
    in_specs = (
        P("row", "col", None),
        P("row", "col", None),
        P("row", "col"),
        P(),
        P(),
        P(),
        P(),
        P(),
        P(),
        P(),
        P(),
    )
    return jax.shard_map(
        local, mesh=mesh, in_specs=in_specs, out_specs=P("row", "col", None), check_vma=False
    )
```
